32 devices in a mesh: tm: 8 (over y, x, core), tile: 4 (over z).
Axes of the slice: x: 2, y: 2, z: 4, core: 2. Of those that a mesh axis runs over, the one named last changes fastest.
Arguments:
- frames: bfloat16 [4096, 32, 1024], P('tm', 'tile')
- bins: int32 [160], replicated, may hold values from 1 to 2047, as said below
- owners: int32 [160, 1], replicated, may hold values from 0 to 3; in each aligned block of 160 rows (0 to 159, 160 to 319, ...) at most 80 rows name the same one
Outputs:
- modes: bfloat16 [320, 4, 32, 1024], P('tile', None, None, 'tm')
- energies: float32 [320], P('tile')
The draws below stay inside these ranges and needn't reach their ends.
Inputs may be any that keep to these rules, and one draw needn't show every extreme that they name: Distinct bins. `owners`: no owner is named by more than 80 bins, a bound that some block reaches.
All inputs are finite; a program needn't handle non-finite values.
Results may differ from the reference program's by a relative error of at most 0.0051.
Values may be sent and summed in bfloat16 or wider, within the bound.
A program may use at most 256 MiB of HBM per device.

```python
import math
import jax
import jax.numpy as jnp
import numpy as np
from jax import lax

FRAMES = 4096
ROWS_DEV = 8
IMG_COLS = 1024
BINS = 160
IMG_ROWS = 32
CAP = 80
SLOTS = 320
N_TILE = 4


def draw_frames(key, part):
    keys = jax.random.split(key, 3)
    row_pos = jnp.arange(IMG_ROWS, dtype=jnp.float32) / max(IMG_ROWS - 1, 1)
    col_pos = jnp.arange(IMG_COLS, dtype=jnp.float32) / max(IMG_COLS - 1, 1)
    trend = (1.0 + 2.0 * row_pos)[:, None] * (1.0 + 2.0 * col_pos)[None, :]
    rough = jnp.exp(jax.random.uniform(keys[0], (IMG_ROWS, IMG_COLS), minval=0.0, maxval=math.log(10.0)))
    scale = 0.1 * trend * rough
    envelope = jnp.exp(jax.random.uniform(keys[1], (FRAMES,), minval=-0.5, maxval=0.5))
    noise = jnp.clip(jax.random.normal(keys[2], (FRAMES, IMG_ROWS, IMG_COLS), jnp.float32), -4.0, 4.0)
    return (noise * envelope[:, None, None] * scale[None, :, :]).astype(jnp.bfloat16)


def draw_bins(key, part):
    inner = jax.random.permutation(key, FRAMES // 2 - 3)[:BINS - 2].astype(jnp.int32) + 2
    ends = jnp.array([1, FRAMES // 2 - 1], dtype=jnp.int32)
    listed = jnp.concatenate([inner, ends])
    return jax.random.permutation(jax.random.fold_in(key, 7), listed).astype(jnp.int32)


def deal_out(key, own, number, rows, amount, top, limit, skew):
    order = jax.random.permutation(key, amount)
    heavy_load, usual = shares(amount, rows * top, limit, skew, True), shares(amount, rows * top, limit, skew, False)
    places = jnp.arange(amount)

    def named(lengths, offset_by):
        used = int((lengths > 0).sum())
        fixed = max(1, used // 4)
        shifted = fixed + (places - fixed + offset_by * (used - fixed)) % max(1, amount - fixed)
        return jnp.zeros((amount,), jnp.int32).at[order[jnp.where(places < fixed, places, shifted)]].set(jnp.asarray(lengths, jnp.int32))

    lengths = jnp.where(number % 4 == 0, named(heavy_load, number // 4), named(usual, number - number // 4 - 1))
    mixed = jax.random.permutation(jax.random.fold_in(own, 3), amount)
    giver, receiver = mixed[0:amount // 2 * 2:2], mixed[1:amount // 2 * 2:2]
    room = jnp.minimum(lengths[giver] - 1, limit - lengths[receiver]) // 2
    room = jnp.where((giver == order[0]) | (receiver == order[0]) | (lengths[receiver] == 0), 0, jnp.maximum(room, 0))
    shifted = jax.random.randint(jax.random.fold_in(own, 4), (amount // 2,), 0, 1 << 20) % (room + 1)
    lengths = lengths.at[giver].add(-shifted).at[receiver].add(shifted)
    items = jnp.searchsorted(jnp.cumsum(lengths), jnp.arange(rows * top), side="right").astype(jnp.int32)
    grid = items.reshape(top, rows).T
    grid = grid[jax.random.permutation(jax.random.fold_in(own, 1), rows)]
    offset_by = jax.random.randint(jax.random.fold_in(own, 2), (rows, 1), 0, top)
    return jnp.take_along_axis(grid, (jnp.arange(top)[None, :] + offset_by) % top, axis=1)


def shares(count, total, most, skew, full):
    weights = [(1 << 20) // math.isqrt(grade ** skew) + 1 for grade in range(1, count + 1)]
    largest = most if full else min(most, max(-(-total // count), total * weights[0] // sum(weights)))
    least = 1 if total - largest >= count - 1 else 0
    counts, spare = [largest] + [least] * (count - 1), total - largest - least * (count - 1)
    while spare > 0:
        free = [i for i in range(1, count) if counts[i] < largest] or [i for i in range(1, count) if counts[i] < most]
        pool, remaining = sum([weights[i] for i in free]), spare
        for i in free:
            addition = min(most - counts[i], max(1, remaining * weights[i] // pool), spare)
            counts[i] = counts[i] + addition
            spare = spare - addition
    return np.array(counts)


def setup_inputs(seed: int = 0) -> dict:
    splits = jax.random.split(jax.random.key(seed), 4)
    frames = draw_frames(jax.random.fold_in(splits[3], 71), 0)
    bins = draw_bins(jax.random.fold_in(splits[3], 71), 0)
    owners_keys = jax.random.split(jax.random.fold_in(splits[2], 1), BINS // BINS)
    owners_turns = jax.random.permutation(jax.random.fold_in(splits[2], 3), BINS // BINS)
    owners = jax.vmap(lambda own, number: deal_out(jax.random.fold_in(splits[2], 2), own, number, BINS, N_TILE, 1, CAP, 2))(owners_keys, owners_turns).reshape((BINS, 1))
    return dict(frames=frames, bins=bins, owners=owners)


def filter_taps():
    position = np.arange(7) - 3.0
    smooth = np.exp(-0.5 * position * position)
    smooth = smooth / smooth.sum()
    slope = position * smooth / np.sum(position * position * smooth)
    return ([float(value) for value in smooth], [float(value) for value in slope])

def separable(field, vertical, horizontal):
    columns = field.shape[2]
    padded = jnp.pad(field, ((0, 0), (0, 0), (3, 3)))
    across = horizontal[0] * padded[:, :, 0:columns]
    for offset in range(1, 7):
        across = across + horizontal[offset] * padded[:, :, offset:offset + columns]
    row_count = field.shape[1] - 6
    result = vertical[0] * across[:, 0:row_count, :]
    for offset in range(1, 7):
        result = result + vertical[offset] * across[:, offset:offset + row_count, :]
    return result

def gradients(strip):
    smooth, slope = filter_taps()
    grad_x = separable(strip, smooth, slope)
    grad_y = separable(strip, slope, smooth)
    return jnp.stack([grad_x, grad_y], axis=1)

def dft_table(bins, first_frame, count, length):
    frame_ids = first_frame + jnp.arange(count, dtype=jnp.int32)
    phase = bins[:, None] * frame_ids[None, :] % length
    angle = phase.astype(jnp.float32) * (2.0 * math.pi / length)
    window_phase = frame_ids.astype(jnp.float32) * (2.0 * math.pi / length)
    window = (0.5 - 0.5 * jnp.cos(window_phase)) / math.sqrt(0.375 * length)
    return jnp.concatenate([jnp.cos(angle) * window[None, :], -jnp.sin(angle) * window[None, :]], axis=0)

def reference(frames, bins, owners):
    table = dft_table(bins, 0, FRAMES, FRAMES)

    def one_strip(strip_id):
        row_ids = strip_id * ROWS_DEV - 3 + jnp.arange(ROWS_DEV + 6, dtype=jnp.int32)
        valid = ((row_ids >= 0) & (row_ids < IMG_ROWS)).astype(jnp.float32)
        strip = jnp.take(frames, jnp.clip(row_ids, 0, IMG_ROWS - 1), axis=1).astype(jnp.float32)
        strip = strip * valid[None, :, None]
        gradient = gradients(strip)
        spectra = jnp.dot(table, gradient.reshape(FRAMES, -1), precision=lax.Precision.HIGHEST)
        return spectra.reshape(2, BINS, 2, ROWS_DEV, IMG_COLS)
    pieces = lax.map(one_strip, jnp.arange(N_TILE, dtype=jnp.int32))
    coeffs = jnp.transpose(pieces, (1, 2, 3, 0, 4, 5)).reshape(2, BINS, 2, IMG_ROWS, IMG_COLS)
    coeffs = coeffs.astype(jnp.bfloat16)
    values = coeffs.astype(jnp.float32)
    energy = lax.optimization_barrier(jnp.sum(values * values, axis=(0, 2, 3, 4))) / (4 * IMG_ROWS * IMG_COLS)
    scale = lax.rsqrt(energy + 1e-06)
    mode = (values * scale[None, :, None, None, None]).astype(jnp.bfloat16)
    mode = jnp.transpose(mode, (1, 0, 2, 3, 4)).reshape(BINS, 4, IMG_ROWS, IMG_COLS)
    owner = owners[:, 0]
    owner_hot = (owner[:, None] == jnp.arange(N_TILE, dtype=jnp.int32)[None, :]).astype(jnp.int32)
    before = jnp.cumsum(owner_hot, axis=0) - owner_hot
    rank = lax.optimization_barrier(jnp.sum(before * owner_hot, axis=1)).astype(jnp.int32)
    slot = (owner * CAP + rank).astype(jnp.int32)
    modes = jnp.zeros((SLOTS, 4, IMG_ROWS, IMG_COLS), jnp.bfloat16).at[slot].set(mode)
    energies = jnp.zeros((SLOTS,), jnp.float32).at[slot].set(energy)
    return (modes, energies)
```

```python
import functools
import math

import jax
import jax.numpy as jnp
import numpy as np
from jax import lax
from jax.experimental import pallas as pl
from jax.experimental.pallas import tpu as pltpu
from jax.sharding import PartitionSpec as P

LANES = 128
REACH = 3
BF16 = jnp.bfloat16
F32 = jnp.float32


def filter_taps():
    position = np.arange(7) - 3.0
    smooth = np.exp(-0.5 * position * position)
    smooth = smooth / smooth.sum()
    slope = position * smooth / np.sum(position * position * smooth)
    return ([float(value) for value in smooth], [float(value) for value in slope])


def dft_table(bins, first_frame, count, length):
    frame_ids = first_frame + jnp.arange(count, dtype=jnp.int32)
    phase = bins[:, None] * frame_ids[None, :] % length
    angle = phase.astype(jnp.float32) * (2.0 * math.pi / length)
    window_phase = frame_ids.astype(jnp.float32) * (2.0 * math.pi / length)
    window = (0.5 - 0.5 * jnp.cos(window_phase)) / math.sqrt(0.375 * length)
    return jnp.concatenate(
        [jnp.cos(angle) * window[None, :], -jnp.sin(angle) * window[None, :]], axis=0
    )


def edge_picker(row_count):
    pick = np.zeros((row_count * LANES, LANES), np.float32)
    for r in range(row_count):
        for e in range(REACH):
            pick[r * LANES + LANES - REACH + e, 6 * r + e] = 1.0
            pick[r * LANES + e, 6 * r + REACH + e] = 1.0
    return pick


def band_matrices(row_count):
    smooth, slope = filter_taps()
    bands = np.zeros((row_count, 2 * LANES, 2 * LANES), np.float32)
    for r in range(row_count):
        for pos, taps in enumerate((slope, smooth)):
            for c in range(LANES):
                for o in range(7):
                    source = c + o - REACH
                    if source < 0:
                        line = LANES + 6 * r + source + REACH
                    elif source >= LANES:
                        line = LANES + 6 * r + REACH + source - LANES
                    else:
                        line = source
                    bands[r, line, pos * LANES + c] = taps[o]
    return bands


def spectra_kernel(row_count, bin_count, blocks, x_ref, t_ref, pick_ref, re_ref, im_ref, wide, cols, edge):
    step = pl.program_id(0)
    frame_count = x_ref.shape[0]
    lane = lax.broadcasted_iota(jnp.int32, (frame_count, LANES), 1)
    from_left = lax.rem(lane, 6) < REACH
    slot = lax.rem(step, 2)
    other = 1 - slot

    @pl.when(step == 0)
    def _():
        edge[...] = jnp.zeros_like(edge)
        cols[...] = jnp.zeros_like(cols)

    left = edge[slot]

    @pl.when(step < blocks)
    def _():
        wide[...] = x_ref[...].astype(F32).reshape(frame_count * row_count, LANES)
        for r in range(row_count):
            cols[slot, :, r * LANES : (r + 1) * LANES] = wide[
                pl.ds(r, frame_count, stride=row_count), :
            ].astype(BF16)
        edge[slot] = jnp.dot(cols[slot], pick_ref[...], preferred_element_type=F32)

    @pl.when(step == blocks)
    def _():
        edge[slot] = jnp.zeros_like(left)

    @pl.when(step > 0)
    def _():
        ends = jnp.where(from_left, left, edge[slot]).astype(BF16)
        table = t_ref[...]
        rows = 2 * bin_count

        def put(r, source):
            y = jnp.dot(table, source, preferred_element_type=F32)
            s = y[:rows] + y[rows:]
            for k in range(source.shape[1] // LANES):
                re_ref[0, r + k] = s[:bin_count, k * LANES : (k + 1) * LANES]
                im_ref[0, r + k] = s[bin_count:, k * LANES : (k + 1) * LANES]

        for r in range(0, row_count, 2):
            put(r, cols[other, :, r * LANES : (r + 2) * LANES])
        put(row_count, ends)


def spectra(frames, table, blocks):
    frame_count, row_count, _ = frames.shape
    bin_count = table.shape[0] // 2
    high = table.astype(BF16)
    low = (table - high.astype(F32)).astype(BF16)
    both = jnp.concatenate([high, low], axis=0)
    pick = jnp.asarray(edge_picker(row_count), BF16)
    out = jax.ShapeDtypeStruct((blocks, row_count + 1, bin_count, LANES), F32)
    out_spec = pl.BlockSpec(
        (1, row_count + 1, bin_count, LANES), lambda i: (jnp.maximum(i - 1, 0), 0, 0, 0)
    )
    return pl.pallas_call(
        functools.partial(spectra_kernel, row_count, bin_count, blocks),
        grid=(blocks + 1,),
        in_specs=[
            pl.BlockSpec(
                (frame_count, row_count, LANES), lambda i: (0, 0, jnp.minimum(i, blocks - 1))
            ),
            pl.BlockSpec(both.shape, lambda i: (0, 0)),
            pl.BlockSpec(pick.shape, lambda i: (0, 0)),
        ],
        out_specs=[out_spec, out_spec],
        out_shape=[out, out],
        scratch_shapes=[
            pltpu.VMEM((frame_count * row_count, LANES), F32),
            pltpu.VMEM((2, frame_count, row_count * LANES), BF16),
            pltpu.VMEM((2, frame_count, LANES), F32),
        ],
        compiler_params=pltpu.CompilerParams(
            dimension_semantics=("arbitrary",), vmem_limit_bytes=40 * 1024 * 1024
        ),
        cost_estimate=pl.CostEstimate(
            flops=2 * 2 * table.size * row_count * blocks * LANES,
            bytes_accessed=frames.size * 2 + 2 * blocks * (row_count + 1) * bin_count * LANES * 4,
            transcendentals=0,
        ),
    )(frames, both, pick)


def filter_kernel(row_count, x_ref, up_ref, down_ref, band_ref, hot_ref, out_ref, sum_ref, across, place):
    smooth, slope = filter_taps()
    bin_count = x_ref.shape[1]
    slots = hot_ref.shape[0]

    def pass_columns(index, cells, ends, r):
        both = jnp.concatenate([cells, ends], axis=1)
        across[index] = jnp.dot(
            both, band_ref[r], precision=lax.Precision.HIGHEST, preferred_element_type=F32
        )

    for r in range(REACH):
        pass_columns(r, up_ref[r], up_ref[REACH], row_count - REACH + r)
        pass_columns(row_count + REACH + r, down_ref[r], down_ref[REACH], r)
    for r in range(row_count):
        pass_columns(REACH + r, x_ref[r], x_ref[row_count], r)

    total = jnp.zeros((bin_count, LANES), F32)
    for k, taps in enumerate((smooth, slope)):
        for r in range(row_count):
            value = jnp.zeros((bin_count, LANES), F32)
            for o in range(7):
                if taps[o] != 0.0:
                    value = value + taps[o] * across[r + o, :, k * LANES : (k + 1) * LANES]
            rounded = value.astype(BF16)
            again = rounded.astype(F32)
            total = total + again * again
            place[pl.ds(r, slots, stride=row_count), :] = jnp.dot(
                hot_ref[...], rounded, preferred_element_type=F32
            )
        out_ref[:, k] = place[...].reshape(slots, row_count, LANES).astype(BF16)
    sum_ref[...] = total


def filter_and_pack(part, up, down, hot):
    row_count = part.shape[0] - 1
    bin_count = part.shape[1]
    slots = hot.shape[0]
    bands = jnp.asarray(band_matrices(row_count))
    return pl.pallas_call(
        functools.partial(filter_kernel, row_count),
        in_specs=[pl.BlockSpec(memory_space=pltpu.VMEM)] * 5,
        out_specs=[pl.BlockSpec(memory_space=pltpu.VMEM)] * 2,
        out_shape=[
            jax.ShapeDtypeStruct((slots, 2, row_count, LANES), BF16),
            jax.ShapeDtypeStruct((bin_count, LANES), F32),
        ],
        scratch_shapes=[
            pltpu.VMEM((row_count + 2 * REACH, bin_count, 2 * LANES), F32),
            pltpu.VMEM((slots * row_count, LANES), F32),
        ],
        compiler_params=pltpu.CompilerParams(vmem_limit_bytes=40 * 1024 * 1024),
        cost_estimate=pl.CostEstimate(
            flops=2 * 6 * 14 * bin_count * 256 * 256, bytes_accessed=8000000, transcendentals=0
        ),
    )(part, up, down, bands, hot)


def slots_of(owners, tile_size, capacity):
    owner = owners[:, 0]
    owner_hot = (owner[:, None] == jnp.arange(tile_size, dtype=jnp.int32)[None, :]).astype(
        jnp.int32
    )
    before = jnp.cumsum(owner_hot, axis=0) - owner_hot
    rank = jnp.sum(before * owner_hot, axis=1)
    slot = owner * capacity + rank
    return jnp.arange(tile_size * capacity, dtype=jnp.int32)[:, None] == slot[None, :]


def plain_pack(part, up, down, left, right, hot):
    smooth, slope = filter_taps()
    row_count = part.shape[0]
    cells = jnp.concatenate([up, part, down], axis=0)
    cells = jnp.concatenate([left, cells, right], axis=2)
    columns = part.shape[2]
    found = []
    for vertical, horizontal in ((smooth, slope), (slope, smooth)):
        across = sum(horizontal[o] * cells[:, :, o : o + columns] for o in range(7))
        found.append(sum(vertical[o] * across[o : o + row_count] for o in range(7)))
    coeffs = jnp.stack(found).astype(BF16)
    again = coeffs.astype(F32)
    total = jnp.sum(again * again, axis=(0, 1))
    packed = jnp.einsum("sb,krbc->skrc", hot, coeffs, preferred_element_type=F32).astype(BF16)
    return packed, total


def shift(cells, axis, by):
    count = lax.axis_size(axis)
    if by > 0:
        pairs = [(i, i + 1) for i in range(count - 1)]
    else:
        pairs = [(i + 1, i) for i in range(count - 1)]
    return lax.ppermute(cells, axis, pairs)


def local(frames, bins, owners):
    frame_count, row_count, columns = frames.shape
    tm_size = lax.axis_size("tm")
    tile_size = lax.axis_size("tile")
    length = frame_count * tm_size
    bin_count = bins.shape[0]
    capacity = 2 * bin_count // tile_size
    first_frame = lax.axis_index("tm") * frame_count
    table = dft_table(bins, first_frame, frame_count, length)
    hot_mask = slots_of(owners, tile_size, capacity)
    hot = hot_mask.astype(BF16)
    features = 4 * row_count * tile_size * columns
    fast = columns == tm_size * LANES and row_count == 8

    if fast:
        terms = spectra(frames, table, tm_size)
    else:
        whole = jnp.einsum(
            "jn,nrc->rjc", table, frames.astype(F32), precision=lax.Precision.HIGHEST
        )
        terms = [whole[:, :bin_count], whole[:, bin_count:]]

    arrived, total = [], 0.0
    for term in terms:
        if fast:
            part = lax.psum_scatter(term, "tm", scatter_dimension=0, tiled=True)
            part = part.reshape(row_count + 1, bin_count, LANES)
            up = shift(part[row_count - REACH :], "tile", 1)
            head = jnp.concatenate([part[:REACH], part[row_count:]], axis=0)
            down = shift(head, "tile", -1)
            packed, squares = filter_and_pack(part, up, down, hot)
        else:
            part = lax.psum_scatter(term, "tm", scatter_dimension=2, tiled=True)
            up = shift(part[row_count - REACH :], "tile", 1)
            down = shift(part[:REACH], "tile", -1)
            tall = jnp.concatenate([up, part, down], axis=0)
            left = shift(tall[:, :, tall.shape[2] - REACH :], "tm", 1)
            right = shift(tall[:, :, :REACH], "tm", -1)
            packed, squares = plain_pack(part, up, down, left, right, hot)
        total = total + squares
        arrived.append(
            lax.all_to_all(packed, "tile", split_axis=0, concat_axis=2, tiled=True)
        )
    energy = lax.psum(jnp.sum(total, axis=1), ("tm", "tile")) / features
    by_slot = jnp.sum(jnp.where(hot_mask, energy[None, :], 0.0), axis=1)
    energy_out = lax.dynamic_slice_in_dim(by_slot, lax.axis_index("tile") * capacity, capacity)
    scale = lax.rsqrt(energy_out + 1e-06)[:, None, None, None]
    mode_out = jnp.concatenate([(a.astype(F32) * scale).astype(BF16) for a in arrived], axis=1)
    return (mode_out, energy_out)


def solution(mesh):
    placed = (P("tm", "tile", None), P(), P())
    return jax.shard_map(
        local,
        mesh=mesh,
        in_specs=placed,
        out_specs=(P("tile", None, None, "tm"), P("tile")),
        check_vma=False,
    )
```

```python
import functools
import math

import jax
import jax.numpy as jnp
import numpy as np
from jax import lax
from jax.experimental import pallas as pl
from jax.experimental.pallas import tpu as pltpu
from jax.sharding import PartitionSpec as P

LANES = 128
REACH = 3
BF16 = jnp.bfloat16
F32 = jnp.float32


def filter_taps():
    position = np.arange(7) - 3.0
    smooth = np.exp(-0.5 * position * position)
    smooth = smooth / smooth.sum()
    slope = position * smooth / np.sum(position * position * smooth)
    return ([float(value) for value in smooth], [float(value) for value in slope])


def dft_table(bins, first_frame, count, length):
    frame_ids = first_frame + jnp.arange(count, dtype=jnp.int32)
    phase = bins[:, None] * frame_ids[None, :] % length
    angle = phase.astype(jnp.float32) * (2.0 * math.pi / length)
    window_phase = frame_ids.astype(jnp.float32) * (2.0 * math.pi / length)
    window = (0.5 - 0.5 * jnp.cos(window_phase)) / math.sqrt(0.375 * length)
    return jnp.concatenate(
        [jnp.cos(angle) * window[None, :], -jnp.sin(angle) * window[None, :]], axis=0
    )


def edge_picker(row_count):
    pick = np.zeros((row_count * LANES, LANES), np.float32)
    for r in range(row_count):
        for e in range(REACH):
            pick[r * LANES + LANES - REACH + e, 6 * r + e] = 1.0
            pick[r * LANES + e, 6 * r + REACH + e] = 1.0
    return pick


def band_matrices(row_count):
    smooth, slope = filter_taps()
    bands = np.zeros((row_count, 2 * LANES, 2 * LANES), np.float32)
    for r in range(row_count):
        for pos, taps in enumerate((slope, smooth)):
            for c in range(LANES):
                for o in range(7):
                    source = c + o - REACH
                    if source < 0:
                        line = LANES + 6 * r + source + REACH
                    elif source >= LANES:
                        line = LANES + 6 * r + REACH + source - LANES
                    else:
                        line = source
                    bands[r, line, pos * LANES + c] = taps[o]
    return bands


def spectra_kernel(row_count, bin_count, blocks, x_ref, t_ref, pick_ref, re_ref, im_ref, wide, cols, edge):
    step = pl.program_id(0)
    frame_count = x_ref.shape[0]
    lane = lax.broadcasted_iota(jnp.int32, (frame_count, LANES), 1)
    from_left = lax.rem(lane, 6) < REACH
    slot = lax.rem(step, 2)
    other = 1 - slot

    @pl.when(step == 0)
    def _():
        edge[...] = jnp.zeros_like(edge)
        cols[...] = jnp.zeros_like(cols)

    left = edge[slot]

    @pl.when(step < blocks)
    def _():
        wide[...] = x_ref[...].astype(F32).reshape(frame_count * row_count, LANES)
        for r in range(row_count):
            cols[slot, :, r * LANES : (r + 1) * LANES] = wide[
                pl.ds(r, frame_count, stride=row_count), :
            ].astype(BF16)
        edge[slot] = jnp.dot(cols[slot], pick_ref[...], preferred_element_type=F32)

    @pl.when(step == blocks)
    def _():
        edge[slot] = jnp.zeros_like(left)

    @pl.when(step > 0)
    def _():
        ends = jnp.where(from_left, left, edge[slot]).astype(BF16)
        table = t_ref[...]
        rows = 2 * bin_count

        def put(r, source):
            y = jnp.dot(table, source, preferred_element_type=F32)
            s = y[:rows] + y[rows:]
            for k in range(source.shape[1] // LANES):
                re_ref[0, r + k] = s[:bin_count, k * LANES : (k + 1) * LANES]
                im_ref[0, r + k] = s[bin_count:, k * LANES : (k + 1) * LANES]

        for r in range(0, row_count, 2):
            put(r, cols[other, :, r * LANES : (r + 2) * LANES])
        put(row_count, ends)


def spectra(frames, table, blocks):
    frame_count, row_count, _ = frames.shape
    bin_count = table.shape[0] // 2
    rounded = lax.reduce_precision(table, 8, 7)
    high = rounded.astype(BF16)
    low = (table - rounded).astype(BF16)
    both = jnp.concatenate([high, low], axis=0)
    pick = jnp.asarray(edge_picker(row_count), BF16)
    out = jax.ShapeDtypeStruct((blocks, row_count + 1, bin_count, LANES), F32)
    out_spec = pl.BlockSpec(
        (1, row_count + 1, bin_count, LANES), lambda i: (jnp.maximum(i - 1, 0), 0, 0, 0)
    )
    return pl.pallas_call(
        functools.partial(spectra_kernel, row_count, bin_count, blocks),
        grid=(blocks + 1,),
        in_specs=[
            pl.BlockSpec(
                (frame_count, row_count, LANES), lambda i: (0, 0, jnp.minimum(i, blocks - 1))
            ),
            pl.BlockSpec(both.shape, lambda i: (0, 0)),
            pl.BlockSpec(pick.shape, lambda i: (0, 0)),
        ],
        out_specs=[out_spec, out_spec],
        out_shape=[out, out],
        scratch_shapes=[
            pltpu.VMEM((frame_count * row_count, LANES), F32),
            pltpu.VMEM((2, frame_count, row_count * LANES), BF16),
            pltpu.VMEM((2, frame_count, LANES), F32),
        ],
        compiler_params=pltpu.CompilerParams(
            dimension_semantics=("arbitrary",), vmem_limit_bytes=40 * 1024 * 1024
        ),
        cost_estimate=pl.CostEstimate(
            flops=2 * 2 * table.size * row_count * blocks * LANES,
            bytes_accessed=frames.size * 2 + 2 * blocks * (row_count + 1) * bin_count * LANES * 4,
            transcendentals=0,
        ),
    )(frames, both, pick)


def scatter_kernel(x_ref, out_ref, pair, half, far, pair_send, pair_recv, far_send, far_recv):
    me = lax.axis_index("tm")
    core = lax.rem(me, 2)
    chip = me // 2
    chip_y, chip_x = chip // 2, lax.rem(chip, 2)
    chips = [lax.rem(chip_y + k // 2, 2) * 2 + lax.rem(chip_x + k % 2, 2) for k in range(4)]
    partner = chip * 2 + 1 - core
    peers = [c * 2 + core for c in chips]

    barrier = pltpu.get_barrier_semaphore()
    for device in [partner] + peers[1:]:
        pl.semaphore_signal(
            barrier, inc=1, device_id={"tm": device}, device_id_type=pl.DeviceIdType.MESH
        )
    pl.semaphore_wait(barrier, 4)

    order = (3, 1, 2, 0)
    first, second = {}, {}
    for k in order:
        first[k] = pltpu.make_async_remote_copy(
            src_ref=x_ref.at[chips[k] * 2 + 1 - core],
            dst_ref=pair.at[k],
            send_sem=pair_send.at[k],
            recv_sem=pair_recv.at[k],
            device_id={"tm": partner},
            device_id_type=pl.DeviceIdType.MESH,
        )
        first[k].start()
    for k in order:
        first[k].wait_recv()
        half[k] = x_ref[chips[k] * 2 + core] + pair[k]
        if k:
            second[k] = pltpu.make_async_remote_copy(
                src_ref=half.at[k],
                dst_ref=far.at[k - 1],
                send_sem=far_send.at[k - 1],
                recv_sem=far_recv.at[k - 1],
                device_id={"tm": peers[k]},
                device_id_type=pl.DeviceIdType.MESH,
            )
            second[k].start()
    for k in (1, 2, 3):
        second[k].wait_recv()
    out_ref[...] = (half[0] + far[0]) + (far[1] + far[2])
    for k in order:
        first[k].wait_send()
    for k in (1, 2, 3):
        second[k].wait_send()


def scatter_sum(term, number):
    block = term.shape[1:]
    return pl.pallas_call(
        scatter_kernel,
        in_specs=[pl.BlockSpec(memory_space=pltpu.VMEM)],
        out_specs=pl.BlockSpec(memory_space=pltpu.VMEM),
        out_shape=jax.ShapeDtypeStruct(block, F32),
        scratch_shapes=[
            pltpu.VMEM((4, *block), F32),
            pltpu.VMEM((4, *block), F32),
            pltpu.VMEM((3, *block), F32),
            pltpu.SemaphoreType.DMA((4,)),
            pltpu.SemaphoreType.DMA((4,)),
            pltpu.SemaphoreType.DMA((3,)),
            pltpu.SemaphoreType.DMA((3,)),
        ],
        compiler_params=pltpu.CompilerParams(
            collective_id=number, has_side_effects=True, vmem_limit_bytes=40 * 1024 * 1024
        ),
    )(term)


def filter_kernel(row_count, x_ref, up_ref, down_ref, band_ref, hot_ref, out_ref, sum_ref, across, place):
    smooth, slope = filter_taps()
    bin_count = x_ref.shape[1]
    slots = hot_ref.shape[0]

    def pass_columns(index, cells, ends, r):
        both = jnp.concatenate([cells, ends], axis=1)
        across[index] = jnp.dot(
            both, band_ref[r], precision=lax.Precision.HIGHEST, preferred_element_type=F32
        )

    for r in range(REACH):
        pass_columns(r, up_ref[r], up_ref[REACH], row_count - REACH + r)
        pass_columns(row_count + REACH + r, down_ref[r], down_ref[REACH], r)
    for r in range(row_count):
        pass_columns(REACH + r, x_ref[r], x_ref[row_count], r)

    total = jnp.zeros((bin_count, LANES), F32)
    for k, taps in enumerate((smooth, slope)):
        for r in range(row_count):
            value = jnp.zeros((bin_count, LANES), F32)
            for o in range(7):
                if taps[o] != 0.0:
                    value = value + taps[o] * across[r + o, :, k * LANES : (k + 1) * LANES]
            rounded = value.astype(BF16)
            again = rounded.astype(F32)
            total = total + again * again
            place[pl.ds(r, slots, stride=row_count), :] = jnp.dot(
                hot_ref[...], rounded, preferred_element_type=F32
            )
        out_ref[:, k] = place[...].reshape(slots, row_count, LANES).astype(BF16)
    sum_ref[...] = total


def filter_and_pack(part, up, down, hot):
    row_count = part.shape[0] - 1
    bin_count = part.shape[1]
    slots = hot.shape[0]
    bands = jnp.asarray(band_matrices(row_count))
    return pl.pallas_call(
        functools.partial(filter_kernel, row_count),
        in_specs=[pl.BlockSpec(memory_space=pltpu.VMEM)] * 5,
        out_specs=[pl.BlockSpec(memory_space=pltpu.VMEM)] * 2,
        out_shape=[
            jax.ShapeDtypeStruct((slots, 2, row_count, LANES), BF16),
            jax.ShapeDtypeStruct((bin_count, LANES), F32),
        ],
        scratch_shapes=[
            pltpu.VMEM((row_count + 2 * REACH, bin_count, 2 * LANES), F32),
            pltpu.VMEM((slots * row_count, LANES), F32),
        ],
        compiler_params=pltpu.CompilerParams(vmem_limit_bytes=40 * 1024 * 1024),
        cost_estimate=pl.CostEstimate(
            flops=2 * 6 * 14 * bin_count * 256 * 256, bytes_accessed=8000000, transcendentals=0
        ),
    )(part, up, down, bands, hot)


def slots_of(owners, tile_size, capacity):
    owner = owners[:, 0]
    owner_hot = (owner[:, None] == jnp.arange(tile_size, dtype=jnp.int32)[None, :]).astype(
        jnp.int32
    )
    before = jnp.cumsum(owner_hot, axis=0) - owner_hot
    rank = jnp.sum(before * owner_hot, axis=1)
    slot = owner * capacity + rank
    return jnp.arange(tile_size * capacity, dtype=jnp.int32)[:, None] == slot[None, :]


def plain_pack(part, up, down, left, right, hot):
    smooth, slope = filter_taps()
    row_count = part.shape[0]
    cells = jnp.concatenate([up, part, down], axis=0)
    cells = jnp.concatenate([left, cells, right], axis=2)
    columns = part.shape[2]
    found = []
    for vertical, horizontal in ((smooth, slope), (slope, smooth)):
        across = sum(horizontal[o] * cells[:, :, o : o + columns] for o in range(7))
        found.append(sum(vertical[o] * across[o : o + row_count] for o in range(7)))
    coeffs = jnp.stack(found).astype(BF16)
    again = coeffs.astype(F32)
    total = jnp.sum(again * again, axis=(0, 1))
    packed = jnp.einsum("sb,krbc->skrc", hot, coeffs, preferred_element_type=F32).astype(BF16)
    return packed, total


def shift(cells, axis, by):
    count = lax.axis_size(axis)
    if by > 0:
        pairs = [(i, i + 1) for i in range(count - 1)]
    else:
        pairs = [(i + 1, i) for i in range(count - 1)]
    return lax.ppermute(cells, axis, pairs)


def local(frames, bins, owners):
    frame_count, row_count, columns = frames.shape
    tm_size = lax.axis_size("tm")
    tile_size = lax.axis_size("tile")
    length = frame_count * tm_size
    bin_count = bins.shape[0]
    capacity = 2 * bin_count // tile_size
    first_frame = lax.axis_index("tm") * frame_count
    table = dft_table(bins, first_frame, frame_count, length)
    hot_mask = slots_of(owners, tile_size, capacity)
    hot = hot_mask.astype(BF16)
    features = 4 * row_count * tile_size * columns
    fast = columns == tm_size * LANES and row_count == 8 and tm_size == 8

    if fast:
        terms = spectra(frames, table, tm_size)
    else:
        whole = jnp.einsum(
            "jn,nrc->rjc", table, frames.astype(F32), precision=lax.Precision.HIGHEST
        )
        terms = [whole[:, :bin_count], whole[:, bin_count:]]

    arrived, total = [], 0.0
    for number, term in enumerate(terms):
        if fast:
            part = scatter_sum(term, number)
            up = shift(part[row_count - REACH :], "tile", 1)
            head = jnp.concatenate([part[:REACH], part[row_count:]], axis=0)
            down = shift(head, "tile", -1)
            packed, squares = filter_and_pack(part, up, down, hot)
        else:
            part = lax.psum_scatter(term, "tm", scatter_dimension=2, tiled=True)
            up = shift(part[row_count - REACH :], "tile", 1)
            down = shift(part[:REACH], "tile", -1)
            tall = jnp.concatenate([up, part, down], axis=0)
            left = shift(tall[:, :, tall.shape[2] - REACH :], "tm", 1)
            right = shift(tall[:, :, :REACH], "tm", -1)
            packed, squares = plain_pack(part, up, down, left, right, hot)
        total = total + squares
        arrived.append(
            lax.all_to_all(packed, "tile", split_axis=0, concat_axis=2, tiled=True)
        )
    energy = lax.psum(jnp.sum(total, axis=1), ("tm", "tile")) / features
    by_slot = jnp.sum(jnp.where(hot_mask, energy[None, :], 0.0), axis=1)
    energy_out = lax.dynamic_slice_in_dim(by_slot, lax.axis_index("tile") * capacity, capacity)
    scale = lax.rsqrt(energy_out + 1e-06)[:, None, None, None]
    mode_out = jnp.concatenate([(a.astype(F32) * scale).astype(BF16) for a in arrived], axis=1)
    return (mode_out, energy_out)


def solution(mesh):
    placed = (P("tm", "tile", None), P(), P())
    return jax.shard_map(
        local,
        mesh=mesh,
        in_specs=placed,
        out_specs=(P("tile", None, None, "tm"), P("tile")),
        check_vma=False,
    )
```

```python
import functools
import math

import jax
import jax.numpy as jnp
import numpy as np
from jax import lax
from jax.experimental import pallas as pl
from jax.experimental.pallas import tpu as pltpu
from jax.sharding import PartitionSpec as P

LANES = 128
REACH = 3
BF16 = jnp.bfloat16
F32 = jnp.float32


def filter_taps():
    position = np.arange(7) - 3.0
    smooth = np.exp(-0.5 * position * position)
    smooth = smooth / smooth.sum()
    slope = position * smooth / np.sum(position * position * smooth)
    return ([float(value) for value in smooth], [float(value) for value in slope])


def dft_table(bins, first_frame, count, length):
    frame_ids = first_frame + jnp.arange(count, dtype=jnp.int32)
    phase = bins[:, None] * frame_ids[None, :] % length
    angle = phase.astype(jnp.float32) * (2.0 * math.pi / length)
    window_phase = frame_ids.astype(jnp.float32) * (2.0 * math.pi / length)
    window = (0.5 - 0.5 * jnp.cos(window_phase)) / math.sqrt(0.375 * length)
    return jnp.concatenate(
        [jnp.cos(angle) * window[None, :], -jnp.sin(angle) * window[None, :]], axis=0
    )


def edge_picker(row_count):
    pick = np.zeros((row_count * LANES, LANES), np.float32)
    for r in range(row_count):
        for e in range(REACH):
            pick[r * LANES + LANES - REACH + e, 6 * r + e] = 1.0
            pick[r * LANES + e, 6 * r + REACH + e] = 1.0
    return pick


def band_matrices(row_count):
    smooth, slope = filter_taps()
    bands = np.zeros((row_count, 2 * LANES, 2 * LANES), np.float32)
    for r in range(row_count):
        for pos, taps in enumerate((slope, smooth)):
            for c in range(LANES):
                for o in range(7):
                    source = c + o - REACH
                    if source < 0:
                        line = LANES + 6 * r + source + REACH
                    elif source >= LANES:
                        line = LANES + 6 * r + REACH + source - LANES
                    else:
                        line = source
                    bands[r, line, pos * LANES + c] = taps[o]
    return bands


def spectra_kernel(row_count, bin_count, blocks, x_ref, t_ref, pick_ref, re_ref, im_ref, wide, cols, edge):
    step = pl.program_id(0)
    frame_count = x_ref.shape[0]
    lane = lax.broadcasted_iota(jnp.int32, (frame_count, LANES), 1)
    from_left = lax.rem(lane, 6) < REACH
    slot = lax.rem(step, 2)
    other = 1 - slot

    @pl.when(step == 0)
    def _():
        edge[...] = jnp.zeros_like(edge)
        cols[...] = jnp.zeros_like(cols)

    left = edge[slot]

    @pl.when(step < blocks)
    def _():
        wide[...] = x_ref[...].astype(F32).reshape(frame_count * row_count, LANES)
        for r in range(row_count):
            cols[slot, :, r * LANES : (r + 1) * LANES] = wide[
                pl.ds(r, frame_count, stride=row_count), :
            ].astype(BF16)
        edge[slot] = jnp.dot(cols[slot], pick_ref[...], preferred_element_type=F32)

    @pl.when(step == blocks)
    def _():
        edge[slot] = jnp.zeros_like(left)

    @pl.when(step > 0)
    def _():
        ends = jnp.where(from_left, left, edge[slot]).astype(BF16)
        table = t_ref[...]
        rows = 2 * bin_count

        def put(r, source):
            y = jnp.dot(table, source, preferred_element_type=F32)
            s = y[:rows] + y[rows:]
            for k in range(source.shape[1] // LANES):
                re_ref[0, r + k] = s[:bin_count, k * LANES : (k + 1) * LANES]
                im_ref[0, r + k] = s[bin_count:, k * LANES : (k + 1) * LANES]

        for r in range(0, row_count, 2):
            put(r, cols[other, :, r * LANES : (r + 2) * LANES])
        put(row_count, ends)


def spectra(frames, table, blocks):
    frame_count, row_count, _ = frames.shape
    bin_count = table.shape[0] // 2
    rounded = lax.reduce_precision(table, 8, 7)
    high = rounded.astype(BF16)
    low = (table - rounded).astype(BF16)
    both = jnp.concatenate([high, low], axis=0)
    pick = jnp.asarray(edge_picker(row_count), BF16)
    out = jax.ShapeDtypeStruct((blocks, row_count + 1, bin_count, LANES), F32)
    out_spec = pl.BlockSpec(
        (1, row_count + 1, bin_count, LANES), lambda i: (jnp.maximum(i - 1, 0), 0, 0, 0)
    )
    return pl.pallas_call(
        functools.partial(spectra_kernel, row_count, bin_count, blocks),
        grid=(blocks + 1,),
        in_specs=[
            pl.BlockSpec(
                (frame_count, row_count, LANES), lambda i: (0, 0, jnp.minimum(i, blocks - 1))
            ),
            pl.BlockSpec(both.shape, lambda i: (0, 0)),
            pl.BlockSpec(pick.shape, lambda i: (0, 0)),
        ],
        out_specs=[out_spec, out_spec],
        out_shape=[out, out],
        scratch_shapes=[
            pltpu.VMEM((frame_count * row_count, LANES), F32),
            pltpu.VMEM((2, frame_count, row_count * LANES), BF16),
            pltpu.VMEM((2, frame_count, LANES), F32),
        ],
        compiler_params=pltpu.CompilerParams(
            dimension_semantics=("arbitrary",), vmem_limit_bytes=40 * 1024 * 1024
        ),
        cost_estimate=pl.CostEstimate(
            flops=2 * 2 * table.size * row_count * blocks * LANES,
            bytes_accessed=frames.size * 2 + 2 * blocks * (row_count + 1) * bin_count * LANES * 4,
            transcendentals=0,
        ),
    )(frames, both, pick)


def scatter_kernel(x_ref, out_ref, pair, half, far, pair_send, pair_recv, far_send, far_recv):
    me = lax.axis_index("tm")
    core = lax.rem(me, 2)
    chip = me // 2
    chip_y, chip_x = chip // 2, lax.rem(chip, 2)
    chips = [lax.rem(chip_y + k // 2, 2) * 2 + lax.rem(chip_x + k % 2, 2) for k in range(4)]
    partner = chip * 2 + 1 - core
    peers = [c * 2 + core for c in chips]

    barrier = pltpu.get_barrier_semaphore()
    for device in [partner] + peers[1:]:
        pl.semaphore_signal(
            barrier, inc=1, device_id={"tm": device}, device_id_type=pl.DeviceIdType.MESH
        )
    pl.semaphore_wait(barrier, 4)

    order = (3, 1, 2, 0)
    first, second = {}, {}
    for k in order:
        first[k] = pltpu.make_async_remote_copy(
            src_ref=x_ref.at[chips[k] * 2 + 1 - core],
            dst_ref=pair.at[k],
            send_sem=pair_send.at[k],
            recv_sem=pair_recv.at[k],
            device_id={"tm": partner},
            device_id_type=pl.DeviceIdType.MESH,
        )
        first[k].start()
    for k in order:
        first[k].wait_recv()
        half[k] = x_ref[chips[k] * 2 + core] + pair[k]
        if k:
            second[k] = pltpu.make_async_remote_copy(
                src_ref=half.at[k],
                dst_ref=far.at[k - 1],
                send_sem=far_send.at[k - 1],
                recv_sem=far_recv.at[k - 1],
                device_id={"tm": peers[k]},
                device_id_type=pl.DeviceIdType.MESH,
            )
            second[k].start()
    for k in (1, 2, 3):
        second[k].wait_recv()
    out_ref[...] = (half[0] + far[0]) + (far[1] + far[2])
    for k in order:
        first[k].wait_send()
    for k in (1, 2, 3):
        second[k].wait_send()


def scatter_sum(term, number):
    block = term.shape[1:]
    return pl.pallas_call(
        scatter_kernel,
        in_specs=[pl.BlockSpec(memory_space=pltpu.VMEM)],
        out_specs=pl.BlockSpec(memory_space=pltpu.VMEM),
        out_shape=jax.ShapeDtypeStruct(block, F32),
        scratch_shapes=[
            pltpu.VMEM((4, *block), F32),
            pltpu.VMEM((4, *block), F32),
            pltpu.VMEM((3, *block), F32),
            pltpu.SemaphoreType.DMA((4,)),
            pltpu.SemaphoreType.DMA((4,)),
            pltpu.SemaphoreType.DMA((3,)),
            pltpu.SemaphoreType.DMA((3,)),
        ],
        compiler_params=pltpu.CompilerParams(
            collective_id=number, has_side_effects=True, vmem_limit_bytes=40 * 1024 * 1024
        ),
    )(term)


def filter_kernel(row_count, x_ref, up_ref, down_ref, band_ref, hot_ref, out_ref, sum_ref, across, place):
    smooth, slope = filter_taps()
    bin_count = x_ref.shape[1]
    slots = hot_ref.shape[0]

    def pass_columns(index, cells, ends, r):
        both = jnp.concatenate([cells, ends], axis=1)
        across[index] = jnp.dot(
            both, band_ref[r], precision=lax.Precision.HIGHEST, preferred_element_type=F32
        )

    for r in range(REACH):
        pass_columns(r, up_ref[r], up_ref[REACH], row_count - REACH + r)
        pass_columns(row_count + REACH + r, down_ref[r], down_ref[REACH], r)
    for r in range(row_count):
        pass_columns(REACH + r, x_ref[r], x_ref[row_count], r)

    total = jnp.zeros((bin_count, LANES), F32)
    for k, taps in enumerate((smooth, slope)):
        for r in range(row_count):
            value = jnp.zeros((bin_count, LANES), F32)
            for o in range(7):
                if taps[o] != 0.0:
                    value = value + taps[o] * across[r + o, :, k * LANES : (k + 1) * LANES]
            rounded = value.astype(BF16)
            again = rounded.astype(F32)
            total = total + again * again
            place[pl.ds(r, slots, stride=row_count), :] = jnp.dot(
                hot_ref[...], rounded, preferred_element_type=F32
            )
        out_ref[:, k] = place[...].reshape(slots, row_count, LANES).astype(BF16)
    sum_ref[...] = total


def filter_and_pack(part, up, down, hot):
    row_count = part.shape[0] - 1
    bin_count = part.shape[1]
    slots = hot.shape[0]
    bands = jnp.asarray(band_matrices(row_count))
    return pl.pallas_call(
        functools.partial(filter_kernel, row_count),
        in_specs=[pl.BlockSpec(memory_space=pltpu.VMEM)] * 5,
        out_specs=[pl.BlockSpec(memory_space=pltpu.VMEM)] * 2,
        out_shape=[
            jax.ShapeDtypeStruct((slots, 2, row_count, LANES), BF16),
            jax.ShapeDtypeStruct((bin_count, LANES), F32),
        ],
        scratch_shapes=[
            pltpu.VMEM((row_count + 2 * REACH, bin_count, 2 * LANES), F32),
            pltpu.VMEM((slots * row_count, LANES), F32),
        ],
        compiler_params=pltpu.CompilerParams(vmem_limit_bytes=40 * 1024 * 1024),
        cost_estimate=pl.CostEstimate(
            flops=2 * 6 * 14 * bin_count * 256 * 256, bytes_accessed=8000000, transcendentals=0
        ),
    )(part, up, down, bands, hot)


def slots_of(owners, tile_size, capacity):
    owner = owners[:, 0]
    owner_hot = (owner[:, None] == jnp.arange(tile_size, dtype=jnp.int32)[None, :]).astype(
        jnp.int32
    )
    before = jnp.cumsum(owner_hot, axis=0) - owner_hot
    rank = jnp.sum(before * owner_hot, axis=1)
    slot = owner * capacity + rank
    return jnp.arange(tile_size * capacity, dtype=jnp.int32)[:, None] == slot[None, :]


def plain_pack(part, up, down, left, right, hot):
    smooth, slope = filter_taps()
    row_count = part.shape[0]
    cells = jnp.concatenate([up, part, down], axis=0)
    cells = jnp.concatenate([left, cells, right], axis=2)
    columns = part.shape[2]
    found = []
    for vertical, horizontal in ((smooth, slope), (slope, smooth)):
        across = sum(horizontal[o] * cells[:, :, o : o + columns] for o in range(7))
        found.append(sum(vertical[o] * across[o : o + row_count] for o in range(7)))
    coeffs = jnp.stack(found).astype(BF16)
    again = coeffs.astype(F32)
    total = jnp.sum(again * again, axis=(0, 1))
    packed = jnp.einsum("sb,krbc->skrc", hot, coeffs, preferred_element_type=F32).astype(BF16)
    return packed, total


def shift(cells, axis, by):
    count = lax.axis_size(axis)
    if by > 0:
        pairs = [(i, i + 1) for i in range(count - 1)]
    else:
        pairs = [(i + 1, i) for i in range(count - 1)]
    return lax.ppermute(cells, axis, pairs)


def local(frames, bins, owners):
    frame_count, row_count, columns = frames.shape
    tm_size = lax.axis_size("tm")
    tile_size = lax.axis_size("tile")
    length = frame_count * tm_size
    bin_count = bins.shape[0]
    capacity = 2 * bin_count // tile_size
    first_frame = lax.axis_index("tm") * frame_count
    table = dft_table(bins, first_frame, frame_count, length)
    hot_mask = slots_of(owners, tile_size, capacity)
    hot = hot_mask.astype(BF16)
    features = 4 * row_count * tile_size * columns
    fast = columns == tm_size * LANES and row_count == 8 and tm_size == 8

    if fast:
        terms = spectra(frames, table, tm_size)
    else:
        whole = jnp.einsum(
            "jn,nrc->rjc", table, frames.astype(F32), precision=lax.Precision.HIGHEST
        )
        terms = [whole[:, :bin_count], whole[:, bin_count:]]

    arrived, total = [], 0.0
    for number, term in enumerate(terms):
        if fast:
            part = scatter_sum(term, number)
            up = shift(part[row_count - REACH :], "tile", 1)
            head = jnp.concatenate([part[:REACH], part[row_count:]], axis=0)
            down = shift(head, "tile", -1)
            packed, squares = filter_and_pack(part, up, down, hot)
        else:
            part = lax.psum_scatter(term, "tm", scatter_dimension=2, tiled=True)
            up = shift(part[row_count - REACH :], "tile", 1)
            down = shift(part[:REACH], "tile", -1)
            tall = jnp.concatenate([up, part, down], axis=0)
            left = shift(tall[:, :, tall.shape[2] - REACH :], "tm", 1)
            right = shift(tall[:, :, :REACH], "tm", -1)
            packed, squares = plain_pack(part, up, down, left, right, hot)
        total = total + squares
        arrived.append(
            lax.all_to_all(packed, "tile", split_axis=0, concat_axis=2, tiled=True)
        )
    energy = lax.psum(lax.psum(jnp.sum(total, axis=1), "tm"), "tile") / features
    by_slot = jnp.sum(jnp.where(hot_mask, energy[None, :], 0.0), axis=1)
    energy_out = lax.dynamic_slice_in_dim(by_slot, lax.axis_index("tile") * capacity, capacity)
    scale = lax.rsqrt(energy_out + 1e-06)[:, None, None, None]
    mode_out = jnp.concatenate([(a.astype(F32) * scale).astype(BF16) for a in arrived], axis=1)
    return (mode_out, energy_out)


def solution(mesh):
    placed = (P("tm", "tile", None), P(), P())
    return jax.shard_map(
        local,
        mesh=mesh,
        in_specs=placed,
        out_specs=(P("tile", None, None, "tm"), P("tile")),
        check_vma=False,
    )
```

```python
import functools
import math

import jax
import jax.numpy as jnp
import numpy as np
from jax import lax
from jax.experimental import pallas as pl
from jax.experimental.pallas import tpu as pltpu
from jax.sharding import PartitionSpec as P

LANES = 128
REACH = 3
BF16 = jnp.bfloat16
F32 = jnp.float32


def filter_taps():
    position = np.arange(7) - 3.0
    smooth = np.exp(-0.5 * position * position)
    smooth = smooth / smooth.sum()
    slope = position * smooth / np.sum(position * position * smooth)
    return ([float(value) for value in smooth], [float(value) for value in slope])


def dft_table(bins, first_frame, count, length):
    frame_ids = first_frame + jnp.arange(count, dtype=jnp.int32)
    phase = bins[:, None] * frame_ids[None, :] % length
    angle = phase.astype(jnp.float32) * (2.0 * math.pi / length)
    window_phase = frame_ids.astype(jnp.float32) * (2.0 * math.pi / length)
    window = (0.5 - 0.5 * jnp.cos(window_phase)) / math.sqrt(0.375 * length)
    return jnp.concatenate(
        [jnp.cos(angle) * window[None, :], -jnp.sin(angle) * window[None, :]], axis=0
    )


def edge_picker(row_count):
    pick = np.zeros((row_count * LANES, LANES), np.float32)
    for r in range(row_count):
        for e in range(REACH):
            pick[r * LANES + LANES - REACH + e, 6 * r + e] = 1.0
            pick[r * LANES + e, 6 * r + REACH + e] = 1.0
    return pick


def band_matrices(row_count):
    smooth, slope = filter_taps()
    bands = np.zeros((row_count, 2 * LANES, 2 * LANES), np.float32)
    for r in range(row_count):
        for pos, taps in enumerate((slope, smooth)):
            for c in range(LANES):
                for o in range(7):
                    source = c + o - REACH
                    if source < 0:
                        line = LANES + 6 * r + source + REACH
                    elif source >= LANES:
                        line = LANES + 6 * r + REACH + source - LANES
                    else:
                        line = source
                    bands[r, line, pos * LANES + c] = taps[o]
    return bands


def spectra_kernel(row_count, bin_count, blocks, x_ref, t_ref, pick_ref, re_ref, im_ref, wide, cols, edge):
    step = pl.program_id(0)
    frame_count = x_ref.shape[0]
    lane = lax.broadcasted_iota(jnp.int32, (frame_count, LANES), 1)
    from_left = lax.rem(lane, 6) < REACH
    slot = lax.rem(step, 2)
    other = 1 - slot

    @pl.when(step == 0)
    def _():
        edge[...] = jnp.zeros_like(edge)
        cols[...] = jnp.zeros_like(cols)

    left = edge[slot]

    @pl.when(step < blocks)
    def _():
        wide[...] = x_ref[...].astype(F32).reshape(frame_count * row_count, LANES)
        for r in range(row_count):
            cols[slot, :, r * LANES : (r + 1) * LANES] = wide[
                pl.ds(r, frame_count, stride=row_count), :
            ].astype(BF16)
        edge[slot] = jnp.dot(cols[slot], pick_ref[...], preferred_element_type=F32)

    @pl.when(step == blocks)
    def _():
        edge[slot] = jnp.zeros_like(left)

    @pl.when(step > 0)
    def _():
        ends = jnp.where(from_left, left, edge[slot]).astype(BF16)
        table = t_ref[...]
        rows = 2 * bin_count

        def put(r, source):
            y = jnp.dot(table, source, preferred_element_type=F32)
            s = y[:rows] + y[rows:]
            for k in range(source.shape[1] // LANES):
                re_ref[0, r + k] = s[:bin_count, k * LANES : (k + 1) * LANES]
                im_ref[0, r + k] = s[bin_count:, k * LANES : (k + 1) * LANES]

        for r in range(0, row_count, 2):
            put(r, cols[other, :, r * LANES : (r + 2) * LANES])
        put(row_count, ends)


def spectra(frames, table, blocks):
    frame_count, row_count, _ = frames.shape
    bin_count = table.shape[0] // 2
    rounded = lax.reduce_precision(table, 8, 7)
    high = rounded.astype(BF16)
    low = (table - rounded).astype(BF16)
    both = jnp.concatenate([high, low], axis=0)
    pick = jnp.asarray(edge_picker(row_count), BF16)
    out = jax.ShapeDtypeStruct((blocks, row_count + 1, bin_count, LANES), F32)
    out_spec = pl.BlockSpec(
        (1, row_count + 1, bin_count, LANES), lambda i: (jnp.maximum(i - 1, 0), 0, 0, 0)
    )
    return pl.pallas_call(
        functools.partial(spectra_kernel, row_count, bin_count, blocks),
        grid=(blocks + 1,),
        in_specs=[
            pl.BlockSpec(
                (frame_count, row_count, LANES), lambda i: (0, 0, jnp.minimum(i, blocks - 1))
            ),
            pl.BlockSpec(both.shape, lambda i: (0, 0)),
            pl.BlockSpec(pick.shape, lambda i: (0, 0)),
        ],
        out_specs=[out_spec, out_spec],
        out_shape=[out, out],
        scratch_shapes=[
            pltpu.VMEM((frame_count * row_count, LANES), F32),
            pltpu.VMEM((2, frame_count, row_count * LANES), BF16),
            pltpu.VMEM((2, frame_count, LANES), F32),
        ],
        compiler_params=pltpu.CompilerParams(
            dimension_semantics=("arbitrary",), vmem_limit_bytes=40 * 1024 * 1024
        ),
        cost_estimate=pl.CostEstimate(
            flops=2 * 2 * table.size * row_count * blocks * LANES,
            bytes_accessed=frames.size * 2 + 2 * blocks * (row_count + 1) * bin_count * LANES * 4,
            transcendentals=0,
        ),
    )(frames, both, pick)


def scatter_kernel(
    x_ref, out_ref, up_ref, down_ref, pair, half, far,
    pair_send, pair_recv, far_send, far_recv, rim_send, rim_recv,
):
    rows = out_ref.shape[0] - 1
    tile = lax.axis_index("tile")
    last = lax.axis_size("tile") - 1
    before, after = jnp.maximum(tile - 1, 0), jnp.minimum(tile + 1, last)
    me = lax.axis_index("tm")
    core = lax.rem(me, 2)
    chip = me // 2
    chip_y, chip_x = chip // 2, lax.rem(chip, 2)
    chips = [lax.rem(chip_y + k // 2, 2) * 2 + lax.rem(chip_x + k % 2, 2) for k in range(4)]
    partner = chip * 2 + 1 - core
    peers = [c * 2 + core for c in chips]

    barrier = pltpu.get_barrier_semaphore()
    for device in [partner] + peers[1:]:
        pl.semaphore_signal(
            barrier, inc=1, device_id={"tm": device}, device_id_type=pl.DeviceIdType.MESH
        )

    @pl.when(tile > 0)
    def _():
        pl.semaphore_signal(
            barrier, inc=1, device_id={"tile": before}, device_id_type=pl.DeviceIdType.MESH
        )

    @pl.when(tile < last)
    def _():
        pl.semaphore_signal(
            barrier, inc=1, device_id={"tile": after}, device_id_type=pl.DeviceIdType.MESH
        )

    pl.semaphore_wait(barrier, 4 + jnp.minimum(tile, 1) + jnp.minimum(last - tile, 1))

    order = (3, 1, 2, 0)
    first, second = {}, {}
    for k in order:
        first[k] = pltpu.make_async_remote_copy(
            src_ref=x_ref.at[chips[k] * 2 + 1 - core],
            dst_ref=pair.at[k],
            send_sem=pair_send.at[k],
            recv_sem=pair_recv.at[k],
            device_id={"tm": partner},
            device_id_type=pl.DeviceIdType.MESH,
        )
        first[k].start()
    for k in order:
        first[k].wait_recv()
        half[k] = x_ref[chips[k] * 2 + core] + pair[k]
        if k:
            second[k] = pltpu.make_async_remote_copy(
                src_ref=half.at[k],
                dst_ref=far.at[k - 1],
                send_sem=far_send.at[k - 1],
                recv_sem=far_recv.at[k - 1],
                device_id={"tm": peers[k]},
                device_id_type=pl.DeviceIdType.MESH,
            )
            second[k].start()
    for k in (1, 2, 3):
        second[k].wait_recv()
    out_ref[...] = (half[0] + far[0]) + (far[1] + far[2])

    def rim(source, target, number, device):
        return pltpu.make_async_remote_copy(
            src_ref=source,
            dst_ref=target,
            send_sem=rim_send.at[number],
            recv_sem=rim_recv.at[number],
            device_id={"tile": device},
            device_id_type=pl.DeviceIdType.MESH,
        )

    tail = rim(out_ref.at[pl.ds(rows - REACH, REACH + 1)], up_ref, 0, after)
    head = rim(out_ref.at[pl.ds(0, REACH)], down_ref.at[pl.ds(0, REACH)], 1, before)
    ends = rim(out_ref.at[pl.ds(rows, 1)], down_ref.at[pl.ds(REACH, 1)], 2, before)

    @pl.when(tile < last)
    def _():
        tail.start()

    @pl.when(tile > 0)
    def _():
        head.start()
        ends.start()
        tail.wait_recv()

    @pl.when(tile == 0)
    def _():
        up_ref[...] = jnp.zeros_like(up_ref)

    @pl.when(tile < last)
    def _():
        head.wait_recv()
        ends.wait_recv()
        tail.wait_send()

    @pl.when(tile == last)
    def _():
        down_ref[...] = jnp.zeros_like(down_ref)

    @pl.when(tile > 0)
    def _():
        head.wait_send()
        ends.wait_send()

    for k in order:
        first[k].wait_send()
    for k in (1, 2, 3):
        second[k].wait_send()


def scatter_sum(term, number):
    block = term.shape[1:]
    return pl.pallas_call(
        scatter_kernel,
        in_specs=[pl.BlockSpec(memory_space=pltpu.VMEM)],
        out_specs=[pl.BlockSpec(memory_space=pltpu.VMEM)] * 3,
        out_shape=[
            jax.ShapeDtypeStruct(block, F32),
            jax.ShapeDtypeStruct((REACH + 1, *block[1:]), F32),
            jax.ShapeDtypeStruct((REACH + 1, *block[1:]), F32),
        ],
        scratch_shapes=[
            pltpu.VMEM((4, *block), F32),
            pltpu.VMEM((4, *block), F32),
            pltpu.VMEM((3, *block), F32),
            pltpu.SemaphoreType.DMA((4,)),
            pltpu.SemaphoreType.DMA((4,)),
            pltpu.SemaphoreType.DMA((3,)),
            pltpu.SemaphoreType.DMA((3,)),
            pltpu.SemaphoreType.DMA((3,)),
            pltpu.SemaphoreType.DMA((3,)),
        ],
        compiler_params=pltpu.CompilerParams(
            collective_id=number, has_side_effects=True, vmem_limit_bytes=40 * 1024 * 1024
        ),
    )(term)


def filter_kernel(row_count, x_ref, up_ref, down_ref, band_ref, hot_ref, out_ref, sum_ref, across, place):
    smooth, slope = filter_taps()
    bin_count = x_ref.shape[1]
    slots = hot_ref.shape[0]

    def pass_columns(index, cells, ends, r):
        both = jnp.concatenate([cells, ends], axis=1)
        across[index] = jnp.dot(
            both, band_ref[r], precision=lax.Precision.HIGHEST, preferred_element_type=F32
        )

    for r in range(REACH):
        pass_columns(r, up_ref[r], up_ref[REACH], row_count - REACH + r)
        pass_columns(row_count + REACH + r, down_ref[r], down_ref[REACH], r)
    for r in range(row_count):
        pass_columns(REACH + r, x_ref[r], x_ref[row_count], r)

    total = jnp.zeros((bin_count, LANES), F32)
    for k, taps in enumerate((smooth, slope)):
        for r in range(row_count):
            value = jnp.zeros((bin_count, LANES), F32)
            for o in range(7):
                if taps[o] != 0.0:
                    value = value + taps[o] * across[r + o, :, k * LANES : (k + 1) * LANES]
            rounded = value.astype(BF16)
            again = rounded.astype(F32)
            total = total + again * again
            place[pl.ds(r, slots, stride=row_count), :] = jnp.dot(
                hot_ref[...], rounded, preferred_element_type=F32
            )
        out_ref[:, k] = place[...].reshape(slots, row_count, LANES).astype(BF16)
    sum_ref[...] = total


def filter_and_pack(part, up, down, hot):
    row_count = part.shape[0] - 1
    bin_count = part.shape[1]
    slots = hot.shape[0]
    bands = jnp.asarray(band_matrices(row_count))
    return pl.pallas_call(
        functools.partial(filter_kernel, row_count),
        in_specs=[pl.BlockSpec(memory_space=pltpu.VMEM)] * 5,
        out_specs=[pl.BlockSpec(memory_space=pltpu.VMEM)] * 2,
        out_shape=[
            jax.ShapeDtypeStruct((slots, 2, row_count, LANES), BF16),
            jax.ShapeDtypeStruct((bin_count, LANES), F32),
        ],
        scratch_shapes=[
            pltpu.VMEM((row_count + 2 * REACH, bin_count, 2 * LANES), F32),
            pltpu.VMEM((slots * row_count, LANES), F32),
        ],
        compiler_params=pltpu.CompilerParams(vmem_limit_bytes=40 * 1024 * 1024),
        cost_estimate=pl.CostEstimate(
            flops=2 * 6 * 14 * bin_count * 256 * 256, bytes_accessed=8000000, transcendentals=0
        ),
    )(part, up, down, bands, hot)


def slots_of(owners, tile_size, capacity):
    owner = owners[:, 0]
    owner_hot = (owner[:, None] == jnp.arange(tile_size, dtype=jnp.int32)[None, :]).astype(
        jnp.int32
    )
    before = jnp.cumsum(owner_hot, axis=0) - owner_hot
    rank = jnp.sum(before * owner_hot, axis=1)
    slot = owner * capacity + rank
    return jnp.arange(tile_size * capacity, dtype=jnp.int32)[:, None] == slot[None, :]


def plain_pack(part, up, down, left, right, hot):
    smooth, slope = filter_taps()
    row_count = part.shape[0]
    cells = jnp.concatenate([up, part, down], axis=0)
    cells = jnp.concatenate([left, cells, right], axis=2)
    columns = part.shape[2]
    found = []
    for vertical, horizontal in ((smooth, slope), (slope, smooth)):
        across = sum(horizontal[o] * cells[:, :, o : o + columns] for o in range(7))
        found.append(sum(vertical[o] * across[o : o + row_count] for o in range(7)))
    coeffs = jnp.stack(found).astype(BF16)
    again = coeffs.astype(F32)
    total = jnp.sum(again * again, axis=(0, 1))
    packed = jnp.einsum("sb,krbc->skrc", hot, coeffs, preferred_element_type=F32).astype(BF16)
    return packed, total


def shift(cells, axis, by):
    count = lax.axis_size(axis)
    if by > 0:
        pairs = [(i, i + 1) for i in range(count - 1)]
    else:
        pairs = [(i + 1, i) for i in range(count - 1)]
    return lax.ppermute(cells, axis, pairs)


def local(frames, bins, owners):
    frame_count, row_count, columns = frames.shape
    tm_size = lax.axis_size("tm")
    tile_size = lax.axis_size("tile")
    length = frame_count * tm_size
    bin_count = bins.shape[0]
    capacity = 2 * bin_count // tile_size
    first_frame = lax.axis_index("tm") * frame_count
    table = dft_table(bins, first_frame, frame_count, length)
    hot_mask = slots_of(owners, tile_size, capacity)
    hot = hot_mask.astype(BF16)
    features = 4 * row_count * tile_size * columns
    fast = columns == tm_size * LANES and row_count == 8 and tm_size == 8

    if fast:
        terms = spectra(frames, table, tm_size)
    else:
        whole = jnp.einsum(
            "jn,nrc->rjc", table, frames.astype(F32), precision=lax.Precision.HIGHEST
        )
        terms = [whole[:, :bin_count], whole[:, bin_count:]]

    arrived, total = [], 0.0
    for number, term in enumerate(terms):
        if fast:
            part, up, down = scatter_sum(term, number)
            packed, squares = filter_and_pack(part, up, down, hot)
        else:
            part = lax.psum_scatter(term, "tm", scatter_dimension=2, tiled=True)
            up = shift(part[row_count - REACH :], "tile", 1)
            down = shift(part[:REACH], "tile", -1)
            tall = jnp.concatenate([up, part, down], axis=0)
            left = shift(tall[:, :, tall.shape[2] - REACH :], "tm", 1)
            right = shift(tall[:, :, :REACH], "tm", -1)
            packed, squares = plain_pack(part, up, down, left, right, hot)
        total = total + squares
        arrived.append(
            lax.all_to_all(packed, "tile", split_axis=0, concat_axis=2, tiled=True)
        )
    energy = lax.psum(lax.psum(jnp.sum(total, axis=1), "tm"), "tile") / features
    by_slot = jnp.sum(jnp.where(hot_mask, energy[None, :], 0.0), axis=1)
    energy_out = lax.dynamic_slice_in_dim(by_slot, lax.axis_index("tile") * capacity, capacity)
    scale = lax.rsqrt(energy_out + 1e-06)[:, None, None, None]
    mode_out = jnp.concatenate([(a.astype(F32) * scale).astype(BF16) for a in arrived], axis=1)
    return (mode_out, energy_out)


def solution(mesh):
    placed = (P("tm", "tile", None), P(), P())
    return jax.shard_map(
        local,
        mesh=mesh,
        in_specs=placed,
        out_specs=(P("tile", None, None, "tm"), P("tile")),
        check_vma=False,
    )
```
